32 devices in a mesh: dp: 16 (over z, y, core), tensor: 2 (over x).
Axes of the slice: x: 2, y: 2, z: 4, core: 2. Of those that a mesh axis runs over, the one named last changes fastest.
Arguments:
- tokens: bfloat16 [16, 1024, 1024], P('dp', 'tensor'), may hold values from -6 to 6
- gain_attn: bfloat16 [1024], P(('dp', 'tensor')), may hold values from 0.25 to 1.75
- gain_ffn: bfloat16 [1024], P(('dp', 'tensor')), may hold values from 0.25 to 1.75
- w_query: bfloat16 [1024, 1024], P('dp', 'tensor'), may hold values from -0.25 to 0.25
- w_key: bfloat16 [1024, 512], P('dp', 'tensor'), may hold values from -0.25 to 0.25
- w_value: bfloat16 [1024, 512], P('dp', 'tensor'), may hold values from -0.1875 to 0.1875
- w_out: bfloat16 [1024, 1024], P('tensor', 'dp'), may hold values from -0.75 to 0.75
- router: bfloat16 [1024, 32], P('dp', 'tensor'), may hold values from -0.09375 to 0.09375
- w_gate: bfloat16 [32, 1024, 512], P('tensor', 'dp'), may hold values from -0.1875 to 0.1875
- w_up: bfloat16 [32, 1024, 512], P('tensor', 'dp'), may hold values from -0.1875 to 0.1875
- w_down: bfloat16 [32, 1024, 512], P('tensor', 'dp'), may hold values from -1 to 1
- cotangent: float32 [16, 1024, 1024], P('dp', 'tensor'), may hold values from -8 to 8
- segments: int32 [16, 1024], P('dp'), may hold values from 0 to 2, as said below
- routing: int32 [16, 1024, 8], P('dp', 'tensor'), may hold values from 0 to 31, all different within a row; in each aligned block of 512 rows (0 to 511, 512 to 1023, ..., all dimensions but the last counted through in order) at most 137 rows name the same one
Outputs:
- output: bfloat16 [16, 1024, 1024], P('dp', 'tensor')
- tokens_grad: bfloat16 [16, 1024, 1024], P('dp', 'tensor')
- grad_gain_attn: float32 [1024], P(('dp', 'tensor'))
- grad_gain_ffn: float32 [1024], P(('dp', 'tensor'))
- grad_w_query: float32 [1024, 1024], P('dp', 'tensor')
- grad_w_key: float32 [1024, 512], P('dp', 'tensor')
- grad_w_value: float32 [1024, 512], P('dp', 'tensor')
- grad_w_out: float32 [1024, 1024], P('tensor', 'dp')
- grad_router: float32 [1024, 32], P('dp', 'tensor')
- grad_w_gate: float32 [32, 1024, 512], P('tensor', 'dp')
- grad_w_up: float32 [32, 1024, 512], P('tensor', 'dp')
- grad_w_down: float32 [32, 1024, 512], P('tensor', 'dp')
The draws below stay inside these ranges and needn't reach their ends.
Inputs may be any that keep to these rules, and one draw needn't show every extreme that they name: `segments`: ids never fall along a sequence; equal ids in a sequence mark one document; each sequence holds three documents of 204 positions or more. `routing`: each row names 8 different experts; in each aligned block of 512 positions of a sequence no expert is named by more than 137 rows.
All inputs are finite; a program needn't handle non-finite values.
Results may differ from the reference program's by a relative error of at most 0.025.
Values may be sent and summed in bfloat16 or wider, within the bound.
No kernel may reach another device: no remote copies, remote signals or barrier semaphores. Data moves between devices by JAX's collectives and lax.ppermute only.
A program may use at most 448 MiB of HBM per device.

```python
import math
import jax
import jax.numpy as jnp
import numpy as np
from jax import lax

D = 1024
H = 16
KV = 8
HD = 64
FF = 512
E = 32
K = 8
LEN = 1024
NSEQ = 16
PIECE = 512
MOST = 137
N_TENSOR = 2


def draw_segments(key, part):
    key = jax.random.fold_in(key, 7)
    first_key, second_key = jax.random.split(key)
    shortest = LEN // 5
    first_cut = jax.random.randint(first_key, (NSEQ, 1), shortest, LEN - 2 * shortest + 1)
    spare = LEN - shortest - first_cut - shortest + 1
    offset = jax.random.randint(second_key, (NSEQ, 1), 0, 1 << 20) % spare
    second_cut = first_cut + shortest + offset
    positions = jnp.arange(LEN, dtype=jnp.int32)[None, :]
    return (positions >= first_cut).astype(jnp.int32) + (positions >= second_cut).astype(jnp.int32)


def strengthened(entries, stream_key, source, target, shards_of, factor):
    owner, partner = [(jnp.arange(entries.shape[dim]) // (entries.shape[dim] // shards_of)).reshape([-1 if axis == dim else 1 for axis in range(entries.ndim)]) for dim in (source, target)]
    chosen = jax.random.permutation(stream_key, shards_of)[partner]
    strong = (owner == chosen) | (owner == (partner + shards_of // 2) % shards_of)
    return jnp.where(strong, factor * entries, entries)


def level_of(own_key, shape, pieces, low, high):
    factor_of = 1.0
    for position, blocks in pieces:
        heights = jax.random.uniform(jax.random.fold_in(jax.random.fold_in(own_key, 6), position), (blocks,), jnp.float32, low / len(pieces), high / len(pieces))
        factor_of = factor_of * jnp.repeat(jnp.exp(heights), shape[position] // blocks).reshape((-1,) + (1,) * (len(shape) - 1 - position))
    return factor_of


def shared_out(rng, own, number, rows, number_of, top, reach, skew):
    order = jax.random.permutation(rng, number_of)
    heavy_load, ordinary = portions_of(number_of, rows * top, reach, skew, True), portions_of(number_of, rows * top, reach, skew, False)
    places = jnp.arange(number_of)

    def named(sizes, offset_by):
        used = int((sizes > 0).sum())
        fixed = max(1, used // 4)
        moved = fixed + (places - fixed + offset_by * (used - fixed)) % max(1, number_of - fixed)
        return jnp.zeros((number_of,), jnp.int32).at[order[jnp.where(places < fixed, places, moved)]].set(jnp.asarray(sizes, jnp.int32))

    sizes = jnp.where(number % 4 == 0, named(heavy_load, number // 4), named(ordinary, number - number // 4 - 1))
    mixed = jax.random.permutation(jax.random.fold_in(own, 3), number_of)
    donor, receiver = mixed[0:number_of // 2 * 2:2], mixed[1:number_of // 2 * 2:2]
    margin = jnp.minimum(sizes[donor] - 1, reach - sizes[receiver]) // 2
    margin = jnp.where((donor == order[0]) | (receiver == order[0]) | (sizes[receiver] == 0), 0, jnp.maximum(margin, 0))
    moved = jax.random.randint(jax.random.fold_in(own, 4), (number_of // 2,), 0, 1 << 20) % (margin + 1)
    sizes = sizes.at[donor].add(-moved).at[receiver].add(moved)
    labels = jnp.searchsorted(jnp.cumsum(sizes), jnp.arange(rows * top), side="right").astype(jnp.int32)
    table = labels.reshape(top, rows).T
    table = table[jax.random.permutation(jax.random.fold_in(own, 1), rows)]
    offset_by = jax.random.randint(jax.random.fold_in(own, 2), (rows, 1), 0, top)
    return jnp.take_along_axis(table, (jnp.arange(top)[None, :] + offset_by) % top, axis=1)


def portions_of(number_of, total, most, slope, full):
    loads = [(1 << 20) // math.isqrt(rank ** slope) + 1 for rank in range(1, number_of + 1)]
    largest = most if full else min(most, max(-(-total // number_of), total * loads[0] // sum(loads)))
    least = 1 if total - largest >= number_of - 1 else 0
    holding, surplus = [largest] + [least] * (number_of - 1), total - largest - least * (number_of - 1)
    while surplus > 0:
        free = [i for i in range(1, number_of) if holding[i] < largest] or [i for i in range(1, number_of) if holding[i] < most]
        mass, remaining = sum([loads[i] for i in free]), surplus
        for i in free:
            extra = min(most - holding[i], max(1, remaining * loads[i] // mass), surplus)
            holding[i] = holding[i] + extra
            surplus = surplus - extra
    return np.array(holding)


def bell_draw(stream_key, dims, spread, most, pieces=(), held_as=jnp.bfloat16):
    array = jax.random.normal(stream_key, dims, jnp.float32) * spread
    if len(pieces) > 0:
        array = level_of(stream_key, dims, pieces, -0.22, 0.18) * array
    return jnp.clip(array, min=-most, max=most).astype(held_as)


def noise_with(key, extent, scale, bound, cuts, heavy, held_as=jnp.bfloat16):
    array = scale * jax.random.normal(key, extent, jnp.float32)
    if cuts:
        array = array * level_of(key, extent, cuts, -0.22, 0.18)
    return jnp.clip(strengthened(array, jax.random.fold_in(key, 3), *heavy), -bound, bound).astype(held_as)


def setup_inputs(seed: int = 0) -> dict:
    splits = jax.random.split(jax.random.key(seed), 15)
    tokens = bell_draw(splits[0], (NSEQ, LEN, D), 1.0, 6.0, ((0, 16), (1, 2)))
    gain_attn = jnp.clip(1.0 + 0.15 * jax.random.normal(splits[1], (D,), jnp.float32), 0.25, 1.75).astype(jnp.bfloat16)
    gain_ffn = jnp.clip(1.0 + 0.15 * jax.random.normal(splits[2], (D,), jnp.float32), 0.25, 1.75).astype(jnp.bfloat16)
    w_query = bell_draw(splits[3], (D, H * HD), (D // 2) ** -0.5, 0.25, ((0, 16), (1, 2)))
    w_key = bell_draw(splits[4], (D, KV * HD), (D // 2) ** -0.5, 0.25, ((0, 16), (1, 2)))
    w_value = bell_draw(splits[5], (D, KV * HD), D ** -0.5, 0.1875, ((0, 16), (1, 2)))
    w_out = bell_draw(splits[6], (H * HD, D), (H * HD // 16) ** -0.5, 0.75, ((0, 2), (1, 16)))
    router = bell_draw(splits[7], (D, E), (4 * D) ** -0.5, 0.09375, ((0, 16), (1, 2)))
    w_gate = bell_draw(splits[8], (E, D, FF), D ** -0.5, 0.1875, ((0, 2), (1, 16)))
    w_up = bell_draw(splits[9], (E, D, FF), D ** -0.5, 0.1875, ((0, 2), (1, 16)))
    w_down = bell_draw(splits[10], (E, D, FF), (FF // 16) ** -0.5, 1.0, ((0, 2), (1, 16)))
    cotangent = noise_with(splits[11], (NSEQ, LEN, D), 1.0, 8.0, ((0, 16), (1, 2)), (0, 2, 16, 2.0), jnp.float32)
    segments = draw_segments(jax.random.fold_in(splits[14], 71), 0)
    routing_keys = jax.random.split(jax.random.fold_in(splits[13], 1), NSEQ * LEN // PIECE)
    routing_turns = jax.random.permutation(jax.random.fold_in(splits[13], 3), NSEQ * LEN // PIECE)
    routing = jax.vmap(lambda own, number: shared_out(jax.random.fold_in(splits[13], 2), own, number, PIECE, E, K, MOST, 1))(routing_keys, routing_turns).reshape((NSEQ, LEN, K))
    return dict(tokens=tokens, gain_attn=gain_attn, gain_ffn=gain_ffn, w_query=w_query, w_key=w_key, w_value=w_value, w_out=w_out, router=router, w_gate=w_gate, w_up=w_up, w_down=w_down, cotangent=cotangent, segments=segments, routing=routing)


epsilon = 1e-06
theta_base = 10000.0
masked_value = -1e+30
highest = lax.Precision.HIGHEST

@jax.custom_vjp
def low(v):
    return lax.optimization_barrier(v.astype(jnp.bfloat16)).astype(jnp.float32)

@jax.custom_vjp
def low_back(v):
    return v

def low_keep(v):
    return (low(v), None)

def low_pass(kept, grad):
    return (grad,)

def back_keep(v):
    return (v, None)

def back_low(kept, grad):
    return (low(grad),)
low.defvjp(low_keep, low_pass)
low_back.defvjp(back_keep, back_low)

def norm_rows(values, gain):
    inverse = lax.rsqrt(lax.optimization_barrier(jnp.mean(values * values, axis=-1, keepdims=True)) + epsilon)
    return values * inverse * gain

def rotate(values):
    half = HD // 2
    frequency = theta_base ** (-(jnp.arange(half, dtype=jnp.float32) * 2.0 / HD))
    angle = jnp.arange(LEN, dtype=jnp.float32)[:, None] * frequency[None, :]
    cosines = jnp.cos(angle)[:, None, :]
    sines = jnp.sin(angle)[:, None, :]
    first = values[..., :half]
    second = values[..., half:]
    return jnp.concatenate([first * cosines - second * sines, second * cosines + first * sines], axis=-1)

def slot_places(routing):
    one_hot = (routing[:, :, None] == jnp.arange(E, dtype=jnp.int32)[None, None, :]).astype(jnp.int32)
    counts = lax.optimization_barrier(jnp.sum(one_hot, axis=1, dtype=jnp.int32)).reshape(N_TENSOR, PIECE, E)
    earlier = (jnp.cumsum(counts, axis=1, dtype=jnp.int32) - counts).reshape(LEN, E)
    slots = jnp.take_along_axis(earlier, routing, axis=1)
    blocks = (jnp.arange(LEN, dtype=jnp.int32) // PIECE)[:, None]
    return (routing * N_TENSOR + blocks) * MOST + slots

def layer(token_rows, gain_attn, gain_ffn, w_query, w_key, w_value, w_out, router, w_gate, w_up, w_down, segments, routing, places):
    normalized_input = low(norm_rows(token_rows, gain_attn))
    queries = low(rotate(low_back(jnp.dot(normalized_input, w_query, precision=highest)).reshape(LEN, H, HD)))
    keys = low(rotate(low_back(jnp.dot(normalized_input, w_key, precision=highest)).reshape(LEN, KV, HD)))
    values = low(low_back(jnp.dot(normalized_input, w_value, precision=highest))).reshape(LEN, KV, HD)
    keys = jnp.repeat(keys, H // KV, axis=1)
    values = jnp.repeat(values, H // KV, axis=1)
    scores = low_back(jnp.einsum('qhd,khd->hqk', queries, keys, precision=highest) * HD ** (-0.5))
    positions = jnp.arange(LEN, dtype=jnp.int32)
    allowed = (positions[:, None] >= positions[None, :]) & (segments[:, None] == segments[None, :])
    scores = jnp.where(allowed[None], scores, masked_value)
    raised = jnp.exp(scores - lax.optimization_barrier(jnp.max(scores, axis=-1, keepdims=True)))
    probs = low(raised / lax.optimization_barrier(jnp.sum(raised, axis=-1, keepdims=True)))
    attention_mixed = jnp.einsum('hqk,khd->qhd', probs, values, precision=highest).reshape(LEN, H * HD)
    attention_mixed = low(low_back(attention_mixed))
    residual = token_rows + low_back(jnp.dot(attention_mixed, w_out, precision=highest))
    normalized_feedforward = low(norm_rows(residual, gain_ffn))
    router_scores = low_back(jnp.dot(normalized_feedforward, router, precision=highest))
    gate_values = jax.nn.softmax(jnp.take_along_axis(router_scores, routing, axis=1), axis=-1)
    flat = places.reshape(-1)
    buffer = jnp.zeros((E * N_TENSOR * MOST, D), jnp.float32).at[flat].set(jnp.repeat(normalized_feedforward, K, axis=0))
    buffer = low_back(buffer.reshape(E, N_TENSOR * MOST, D))
    gate_pre = low_back(jnp.einsum('erd,edf->erf', buffer, w_gate, precision=highest))
    up_pre = low_back(jnp.einsum('erd,edf->erf', buffer, w_up, precision=highest))
    hidden = low(jax.nn.silu(gate_pre) * up_pre)
    produced = low(low_back(jnp.einsum('erf,edf->erd', hidden, w_down, precision=highest)))
    picked = produced.reshape(-1, D)[places]
    return residual + jnp.einsum('lk,lkd->ld', gate_values, picked, precision=highest)

def reference(tokens, gain_attn, gain_ffn, w_query, w_key, w_value, w_out, router, w_gate, w_up, w_down, cotangent, segments, routing):
    params = tuple((weight.astype(jnp.float32) for weight in (gain_attn, gain_ffn, w_query, w_key, w_value, w_out, router, w_gate, w_up, w_down)))

    def step(totals, batch):
        batch_tokens, batch_grad, batch_segments, batch_routing = batch
        places = slot_places(batch_routing)

        def forward(token_rows, *weights):
            return layer(token_rows, *weights, batch_segments, batch_routing, places)
        result, pullback = jax.vjp(forward, batch_tokens.astype(jnp.float32), *params)
        grads = pullback(batch_grad.astype(jnp.float32))
        totals = tuple((total + grad for total, grad in zip(totals, grads[1:])))
        return (totals, (result.astype(jnp.bfloat16), grads[0].astype(jnp.bfloat16)))
    start = tuple((jnp.zeros(weight.shape, jnp.float32) for weight in params))
    totals, (outputs, token_grads) = lax.scan(step, start, (tokens, cotangent, segments, routing))
    return (outputs, token_grads, totals[0], totals[1], totals[2], totals[3], totals[4], totals[5], totals[6], totals[7], totals[8], totals[9])
```

```python
import functools
import math

import jax
import jax.numpy as jnp
from jax import lax
from jax.experimental import pallas as pl
from jax.experimental.pallas import tpu as pltpu
from jax.sharding import PartitionSpec as P


HD = 64
K = 8


epsilon = 1e-06
theta_base = 10000.0
masked_value = -1e30


def rotary_tables(length, head_width):
    half = head_width // 2
    frequency = theta_base ** (-(jnp.arange(half, dtype=jnp.float32) * 2.0 / head_width))
    angle = jnp.arange(length, dtype=jnp.float32)[:, None] * frequency[None, :]
    return (jnp.cos(angle)[:, None, :], jnp.sin(angle)[:, None, :])


def rotate(values, cosines, sines):
    half = values.shape[-1] // 2
    first = values[..., :half]
    second = values[..., half:]
    return jnp.concatenate(
        [first * cosines - second * sines, second * cosines + first * sines], axis=-1
    )


def rotate_back(grads, cosines, sines):
    half = grads.shape[-1] // 2
    first = grads[..., :half]
    second = grads[..., half:]
    return jnp.concatenate(
        [first * cosines + second * sines, second * cosines - first * sines], axis=-1
    )


f32 = jnp.float32
bf16 = jnp.bfloat16
vmem_bytes = 56 * 1024 * 1024
DEPTH = 4
CHUNKS = 4


def dot(a, b, left=1, right=0):
    return lax.dot_general(a, b, (((left,), (right,)), ((), ())), preferred_element_type=f32)


def expert_kernel(
    own_ref, rank_ref, gate_ref, x_ref, c_ref, wg_ref, wu_ref, wd_ref, mix_ref, back_ref, gg_ref, keep_ref, send_ref
):
    blocks, cap = mix_ref.shape[1], mix_ref.shape[2]
    length = rank_ref.shape[-1]
    width = x_ref.shape[1]
    hidden_width = wg_ref.shape[-1]
    groups, rows_each = wg_ref.shape[0], wg_ref.shape[3]
    wg = wg_ref[...].reshape(width, hidden_width)
    wu = wu_ref[...].reshape(width, hidden_width)
    wd = wd_ref[...].reshape(width, hidden_width)
    slots = lax.broadcasted_iota(jnp.int32, (cap, length), 0)
    picks, rows, grads, gate_rows = [], [], [], []
    for b in range(blocks):
        pick = slots == rank_ref[0, b]
        one_hot = pick.astype(f32).astype(bf16)
        picks.append(pick)
        rows.append(dot(one_hot, x_ref[b * length : (b + 1) * length, :]).astype(bf16))
        grads.append(dot(one_hot, c_ref[b * length : (b + 1) * length, :]))
        gate_rows.append(jnp.sum(jnp.where(pick, gate_ref[0, b], 0.0), axis=1, keepdims=True))
    buffer = jnp.concatenate(rows, axis=0)
    cotangent = jnp.concatenate(grads, axis=0)
    gate_row = jnp.concatenate(gate_rows, axis=0)
    gate_pre = dot(buffer, wg)
    up_pre = dot(buffer, wu)
    sigmoid = 1.0 / (1.0 + jnp.exp(-gate_pre))
    silu = gate_pre * sigmoid
    hidden = (silu * up_pre).astype(bf16)
    produced = dot(hidden, wd, 1, 1)
    gates_grad = jnp.sum(cotangent * produced, axis=1, keepdims=True)
    mix = (gate_row * produced).astype(bf16)
    picked_grad = (gate_row * cotangent).astype(bf16)
    hidden_grad = dot(picked_grad, wd)
    gate_grad = (hidden_grad * up_pre * (sigmoid * (1.0 + gate_pre * (1.0 - sigmoid)))).astype(bf16)
    up_grad = (hidden_grad * silu).astype(bf16)
    back = (dot(gate_grad, wg, 1, 1) + dot(up_grad, wu, 1, 1)).astype(bf16)
    for b in range(blocks):
        mix_ref[0, b] = mix[b * cap : (b + 1) * cap]
        back_ref[0, b] = back[b * cap : (b + 1) * cap]
        gg_ref[0, b] = jnp.sum(
            jnp.where(picks[b], gates_grad[b * cap : (b + 1) * cap], 0.0), axis=0, keepdims=True
        )
    own_core, own_row = own_ref[0], own_ref[1]
    row_count = groups // 2 // DEPTH
    for kind, (a, g) in enumerate(((buffer, gate_grad), (buffer, up_grad), (picked_grad, hidden))):
        total = dot(a, g, 0, 0).astype(bf16).reshape(groups, rows_each, hidden_width)
        for device in range(groups):
            z, y, core = device // (2 * row_count), device // 2 % row_count, device % 2
            place = (y ^ own_row) * DEPTH + z

            @pl.when(core == own_core)
            def keep():
                keep_ref[place, kind, 0] = total[device]

            @pl.when(core != own_core)
            def send():
                send_ref[place, kind, 0] = total[device]


def experts(own, rank, gates, tokens, cotangent, weights, capacity):
    count, blocks, _, length = rank.shape
    width = tokens.shape[1]
    groups, _, _, rows_each, hidden_width = weights.shape
    half = groups // 2
    whole = lambda e, own: (0, 0)
    each = lambda e, own: (e, 0, 0, 0)
    weight = lambda kind: pl.BlockSpec(
        (groups, 1, 1, rows_each, hidden_width), lambda e, own: (0, kind, e, 0, 0)
    )
    grad = pl.BlockSpec((half, 3, 1, rows_each, hidden_width), lambda e, own: (0, 0, e, 0, 0))
    row = pl.BlockSpec((1, blocks, 1, length), each)
    moved = pl.BlockSpec((1, blocks, capacity, width), each)
    slots = jax.ShapeDtypeStruct((count, blocks, capacity, width), bf16)
    grads = jax.ShapeDtypeStruct((half, 3, count, rows_each, hidden_width), bf16)
    all_rows = count * blocks * capacity
    return pl.pallas_call(
        expert_kernel,
        grid_spec=pltpu.PrefetchScalarGridSpec(
            num_scalar_prefetch=1,
            grid=(count,),
            in_specs=[
                row,
                row,
                pl.BlockSpec(tokens.shape, whole),
                pl.BlockSpec(tokens.shape, whole),
                weight(0),
                weight(1),
                weight(2),
            ],
            out_specs=[moved, moved, row, grad, grad],
        ),
        out_shape=[slots, slots, jax.ShapeDtypeStruct(rank.shape, f32), grads, grads],
        compiler_params=pltpu.CompilerParams(vmem_limit_bytes=vmem_bytes),
        cost_estimate=pl.CostEstimate(
            flops=2 * all_rows * width * (9 * hidden_width + 2 * length),
            bytes_accessed=2 * 2 * 3 * count * width * hidden_width + 8 * all_rows * width,
            transcendentals=all_rows * hidden_width,
        ),
    )(own, rank, gates, tokens, cotangent, weights, weights, weights)


def combine_kernel(rank_ref, *refs):
    parts, mix_out, back_out = refs[:-2], refs[-2], refs[-1]
    half = len(parts) // 2
    count, _, cap, tile = parts[0].shape
    length = rank_ref.shape[-1]
    slots = lax.broadcasted_iota(jnp.int32, (cap, length), 0)
    for sources, target in ((parts[:half], mix_out), (parts[half:], back_out)):
        total = jnp.zeros((length, tile), f32)
        for i, source in enumerate(sources):
            pick = jnp.concatenate(
                [
                    (slots == rank_ref[i * count + e, 0]).astype(f32).astype(bf16)
                    for e in range(count)
                ],
                axis=0,
            )
            total = total + dot(pick, source[...].reshape(count * cap, tile), 0, 0)
        target[...] = total.astype(bf16)


def combine(rank, mixes, backs):
    experts_here, blocks, _, length = rank.shape
    count, _, cap, width = mixes[0].shape
    tile = min(512, width)
    source = pl.BlockSpec((count, 1, cap, tile), lambda b, n: (0, b, 0, n))
    target = pl.BlockSpec((length, tile), lambda b, n: (b, n))
    shape = jax.ShapeDtypeStruct((blocks * length, width), bf16)
    rows = experts_here * cap * blocks
    return pl.pallas_call(
        combine_kernel,
        grid=(blocks, width // tile),
        in_specs=[pl.BlockSpec((experts_here, 1, 1, length), lambda b, n: (0, b, 0, 0))]
        + [source] * (2 * len(mixes)),
        out_specs=[target, target],
        out_shape=[shape, shape],
        compiler_params=pltpu.CompilerParams(vmem_limit_bytes=vmem_bytes),
        cost_estimate=pl.CostEstimate(
            flops=4 * rows * length * width, bytes_accessed=4 * rows * width, transcendentals=0
        ),
    )(rank, *mixes, *backs)


def gather_tensor(piece):
    if lax.axis_size("tensor") != 2:
        return lax.all_gather(piece, "tensor", axis=0, tiled=True)
    other = lax.ppermute(piece, "tensor", [(0, 1), (1, 0)])
    first = lax.axis_index("tensor") == 0
    return jnp.concatenate([jnp.where(first, piece, other), jnp.where(first, other, piece)], axis=0)


def scatter_tensor(whole):
    if lax.axis_size("tensor") != 2:
        return lax.psum_scatter(
            whole.astype(bf16), "tensor", scatter_dimension=0, tiled=True
        ).astype(f32)
    length = whole.shape[0] // 2
    here = lax.axis_index("tensor")
    other = lax.dynamic_slice_in_dim(whole, (1 - here) * length, length, 0).astype(bf16)
    own = lax.dynamic_slice_in_dim(whole, here * length, length, 0)
    return own.astype(f32) + lax.ppermute(other, "tensor", [(0, 1), (1, 0)]).astype(f32)


def gather_experts(piece):
    parts, count, length = piece.shape
    if parts != 2:
        moved = lax.all_to_all(piece, "tensor", split_axis=0, concat_axis=0, tiled=True)
        return moved.reshape(parts * count, length)
    here = lax.axis_index("tensor")
    own = lax.dynamic_index_in_dim(piece, here, 0, keepdims=False)
    other = lax.dynamic_index_in_dim(piece, 1 - here, 0, keepdims=False)
    other = lax.ppermute(other, "tensor", [(0, 1), (1, 0)])
    first = here == 0
    return jnp.concatenate([jnp.where(first, own, other), jnp.where(first, other, own)], axis=0)


def sum_weights(keep, send):
    groups = lax.axis_size("dp")
    received = lax.ppermute(send, "dp", [(i, i ^ 1) for i in range(groups)])
    total = keep.astype(f32) + received.astype(f32)
    distance = groups // DEPTH // 2
    while distance > 1:
        distance //= 2
        half = total.shape[0] // 2
        sent = total[half:].astype(bf16)
        received = lax.ppermute(sent, "dp", [(i, i ^ (2 * distance)) for i in range(groups)])
        total = total[:half] + received.astype(f32)
    plane = groups // DEPTH
    lines = [[z * plane + i for z in range(DEPTH)] for i in range(plane)]
    return lax.psum_scatter(
        total.astype(bf16), "dp", scatter_dimension=0, axis_index_groups=lines, tiled=False
    )


def on_device(
    tokens,
    gain_attn,
    gain_ffn,
    w_query,
    w_key,
    w_value,
    w_out,
    router,
    w_gate,
    w_up,
    w_down,
    cotangent,
    segments,
    routing,
):
    _, local_len, width = tokens.shape
    parts = lax.axis_size("tensor")
    groups = lax.axis_size("dp")
    here = lax.axis_index("tensor")
    full_len = local_len * parts
    heads_here = w_query.shape[1] // HD
    kv_here = w_key.shape[1] // HD
    group_size = heads_here // kv_here
    experts_here = w_gate.shape[0]
    all_experts = experts_here * parts
    capacity = 17 * local_len * K // (16 * all_experts) + 1
    capacity = -(-capacity // 16) * 16
    gain_len = gain_attn.shape[0]
    rows_each = width // groups
    query_cols = heads_here * HD
    kv_cols = kv_here * HD
    scale = 1.0 / math.sqrt(HD)
    block = min(512, full_len)
    tokens = tokens[0]
    cotangent = cotangent[0]
    segments = segments[0]

    columns = jnp.zeros((rows_each, 2), bf16)
    columns = lax.dynamic_update_slice(
        columns, jnp.stack([gain_attn, gain_ffn], axis=1), (here * gain_len, 0)
    )
    small = gather_tensor(jnp.concatenate([router, columns], axis=1)[None])
    router_rows = jnp.transpose(small[:, :, :experts_here], (1, 0, 2)).reshape(rows_each, all_experts)
    gains_rows = jnp.sum(small[:, :, experts_here:].astype(f32), axis=0).astype(bf16)
    attention_piece = jnp.concatenate(
        [w_query, w_key, w_value, jnp.transpose(w_out), router_rows, gains_rows], axis=1
    )
    piece_cols = attention_piece.shape[1]
    attention_piece = jnp.pad(attention_piece, ((0, 0), (0, -piece_cols % 128)))
    attention_weights = lax.all_gather(attention_piece, "dp", axis=0, tiled=True)
    qkv_cols = query_cols + 2 * kv_cols
    qkv_weights = attention_weights[:, :qkv_cols]
    out_turned = attention_weights[:, qkv_cols : qkv_cols + query_cols]
    rest = attention_weights[:, qkv_cols + query_cols :]
    router_complete = rest[:, :all_experts]
    gain_one = rest[:, all_experts].astype(f32)
    gain_two = rest[:, all_experts + 1].astype(f32)

    chunk = max(1, experts_here // CHUNKS)
    expert_weights = [
        lax.all_gather(
            jnp.stack([w[first : first + chunk] for w in (w_gate, w_up, w_down)]), "dp", axis=0
        )
        for first in range(0, experts_here, chunk)
    ]

    tokens_all = gather_tensor(tokens)
    cotangent_all = gather_tensor(cotangent.astype(bf16))
    routing_all = gather_tensor(routing[0])
    tokens_wide = tokens_all.astype(f32)
    inverse_one = lax.rsqrt(jnp.mean(tokens_wide * tokens_wide, axis=-1, keepdims=True) + epsilon)
    normalized_input = (tokens_wide * inverse_one * gain_one).astype(bf16)
    cosines, sines = rotary_tables(full_len, HD)
    qkv = dot(normalized_input, qkv_weights)
    queries = rotate(
        qkv[:, :query_cols].reshape(full_len, heads_here, HD), cosines, sines
    ).astype(bf16)
    keys = rotate(
        qkv[:, query_cols : query_cols + kv_cols].reshape(full_len, kv_here, HD), cosines, sines
    ).astype(bf16)
    values = qkv[:, query_cols + kv_cols :].reshape(full_len, kv_here, HD).astype(bf16)
    positions = jnp.arange(full_len, dtype=jnp.int32)

    def allowed_block(first, last):
        rows = positions[first : first + block]
        causal = rows[:, None] >= positions[None, :last]
        same = segments[first : first + block, None] == segments[None, :last]
        return causal & same

    head_outputs = []
    log_totals = []
    for head in range(heads_here):
        keys_head = keys[:, head // group_size]
        values_head = values[:, head // group_size]
        out_blocks = []
        total_blocks = []
        for first in range(0, full_len, block):
            last = min(first + block, full_len)
            score = dot(queries[first:last, head], keys_head[:last], 1, 1) * scale
            score = jnp.where(allowed_block(first, last), score, masked_value)
            top = jnp.max(score, axis=-1, keepdims=True)
            raised = jnp.exp(score - top)
            total = jnp.sum(raised, axis=-1, keepdims=True)
            probs = (raised / total).astype(bf16)
            out_blocks.append(dot(probs, values_head[:last]).astype(bf16))
            total_blocks.append(top + jnp.log(total))
        head_outputs.append(jnp.concatenate(out_blocks, axis=0))
        log_totals.append(jnp.concatenate(total_blocks, axis=0))
    mixed = jnp.concatenate(head_outputs, axis=-1)
    attended = scatter_tensor(dot(mixed, out_turned, 1, 1))
    tokens_local = tokens.astype(f32)
    residual = tokens_local + attended
    inverse_two = lax.rsqrt(jnp.mean(residual * residual, axis=-1, keepdims=True) + epsilon)
    normalized = (residual * inverse_two * gain_two).astype(bf16)
    normalized_all = gather_tensor(normalized)

    logits = dot(normalized_all, router_complete)
    named = jnp.any(
        routing_all[:, :, None] == jnp.arange(all_experts, dtype=jnp.int32), axis=1
    )
    chosen = jnp.where(named, logits, masked_value)
    raised = jnp.where(named, jnp.exp(chosen - jnp.max(chosen, axis=-1, keepdims=True)), 0.0)
    gates = raised / jnp.sum(raised, axis=-1, keepdims=True)
    earlier = jnp.arange(local_len)[:, None] < jnp.arange(local_len)[None, :]
    named_here = lax.dynamic_slice_in_dim(named, here * experts_here, experts_here, 1)
    named_here = named_here.reshape(parts, local_len, experts_here)
    slots = jnp.einsum(
        "bte,ts->ebs", named_here.astype(bf16), earlier.astype(bf16), preferred_element_type=f32
    ).astype(jnp.int32)
    rank = jnp.where(jnp.transpose(named_here, (2, 0, 1)), slots, -1)[:, :, None, :]
    gates_here = lax.dynamic_slice_in_dim(gates, here * experts_here, experts_here, 1)
    gates_here = jnp.transpose(gates_here).reshape(experts_here, parts, 1, local_len)

    place = lax.axis_index("dp")
    own = jnp.stack([place % 2, place // 2 % (groups // 2 // DEPTH)]).astype(jnp.int32)
    mixes, backs, gate_sums, weight_sums = [], [], [], []
    for i, weights in enumerate(expert_weights):
        span = slice(i * chunk, (i + 1) * chunk)
        mix, back, gate_sum, keep, send = experts(
            own, rank[span], gates_here[span], normalized_all, cotangent_all, weights, capacity
        )
        mixes.append(mix)
        backs.append(back)
        gate_sums.append(gate_sum)
        weight_sums.append(sum_weights(keep, send))
    mix_part, back_part = combine(rank, mixes, backs)
    gate_sums = jnp.concatenate(gate_sums, axis=0).reshape(experts_here, parts, local_len)
    gates_grad = jnp.transpose(
        gather_experts(jnp.transpose(gate_sums, (1, 0, 2))), (1, 0)
    )
    ffn_grad = scatter_tensor(back_part)
    gates_local = lax.dynamic_slice_in_dim(gates, here * local_len, local_len, 0)
    selected_grad = gates_local * (
        gates_grad - jnp.sum(gates_local * gates_grad, axis=-1, keepdims=True)
    )
    logits_grad = selected_grad.astype(bf16)
    ffn_grad = ffn_grad + dot(logits_grad, router_complete, 1, 1)
    router_part = dot(normalized, logits_grad, 0, 0)
    hat_two = residual * inverse_two
    scaled_two = ffn_grad * gain_two
    residual_grad = cotangent + inverse_two * (
        scaled_two - hat_two * jnp.mean(hat_two * scaled_two, axis=-1, keepdims=True)
    )
    gain_two_part = jnp.sum(ffn_grad * hat_two, axis=0)
    gradient = gather_tensor(residual_grad.astype(bf16))
    output = (residual + scatter_tensor(mix_part)).astype(bf16)

    mixed_grad = dot(gradient, out_turned).astype(bf16)
    out_grad_turned = dot(gradient, mixed, 0, 0)
    query_grads = []
    key_grads = [jnp.zeros((full_len, HD), f32) for _ in range(kv_here)]
    value_grads = [jnp.zeros((full_len, HD), f32) for _ in range(kv_here)]
    for head in range(heads_here):
        group = head // group_size
        keys_head = keys[:, group]
        values_head = values[:, group]
        blocks_grad = []
        for first in range(0, full_len, block):
            last = min(first + block, full_len)
            query_block = queries[first:last, head]
            score = dot(query_block, keys_head[:last], 1, 1) * scale
            score = jnp.where(allowed_block(first, last), score, masked_value)
            probs = jnp.exp(score - log_totals[head][first:last])
            out_grad_block = mixed_grad[first:last, head * HD : (head + 1) * HD]
            prob_grad = dot(out_grad_block, values_head[:last], 1, 1)
            delta = jnp.sum(probs * prob_grad, axis=-1, keepdims=True)
            score_grad = (probs * (prob_grad - delta)).astype(bf16)
            blocks_grad.append(dot(score_grad, keys_head[:last]) * scale)
            key_grads[group] = (
                key_grads[group].at[:last].add(dot(score_grad, query_block, 0, 0) * scale)
            )
            value_grads[group] = (
                value_grads[group].at[:last].add(dot(probs.astype(bf16), out_grad_block, 0, 0))
            )
        query_grads.append(jnp.concatenate(blocks_grad, axis=0))
    query_gradient = rotate_back(jnp.stack(query_grads, axis=1), cosines, sines)
    key_gradient = rotate_back(jnp.stack(key_grads, axis=1), cosines, sines)
    qkv_gradient = jnp.concatenate(
        [
            query_gradient.astype(bf16).reshape(full_len, query_cols),
            key_gradient.astype(bf16).reshape(full_len, kv_cols),
            jnp.stack(value_grads, axis=1).astype(bf16).reshape(full_len, kv_cols),
        ],
        axis=1,
    )
    normed_grad = dot(qkv_gradient, qkv_weights, 1, 1)
    gain_one_part = jnp.sum(normed_grad * tokens_wide * inverse_one, axis=0)
    qkv_weight_grad = dot(normalized_input, qkv_gradient, 0, 0)
    row_sum = scatter_tensor(normed_grad)
    inverse_local = lax.rsqrt(
        jnp.mean(tokens_local * tokens_local, axis=-1, keepdims=True) + epsilon
    )
    hat_one = tokens_local * inverse_local
    scaled_one = row_sum * gain_one
    tokens_grad = (
        residual_grad
        + inverse_local
        * (scaled_one - hat_one * jnp.mean(hat_one * scaled_one, axis=-1, keepdims=True))
    ).astype(bf16)
    attention_grads = jnp.concatenate(
        [
            qkv_weight_grad.astype(bf16),
            out_grad_turned.astype(bf16),
            router_part.astype(bf16),
            jnp.stack([gain_one_part, gain_two_part], axis=1).astype(bf16),
        ],
        axis=1,
    )
    attention_grads = jnp.pad(attention_grads, ((0, 0), (0, -piece_cols % 128)))
    summed = lax.psum_scatter(attention_grads, "dp", scatter_dimension=0, tiled=True)
    small_sum = lax.psum(summed[:, qkv_cols + query_cols :].astype(f32), "tensor")
    summed = summed.astype(f32)
    router_shard = lax.dynamic_slice_in_dim(small_sum, here * experts_here, experts_here, 1)
    gain_shard = lax.dynamic_slice_in_dim(small_sum, here * gain_len, gain_len, 0)
    weight_grads = jnp.concatenate(weight_sums, axis=1).astype(f32)
    return (
        output[None],
        tokens_grad[None],
        gain_shard[:, all_experts],
        gain_shard[:, all_experts + 1],
        summed[:, :query_cols],
        summed[:, query_cols : query_cols + kv_cols],
        summed[:, query_cols + kv_cols : qkv_cols],
        jnp.transpose(summed[:, qkv_cols : qkv_cols + query_cols]),
        router_shard,
        weight_grads[0],
        weight_grads[1],
        weight_grads[2],
    )


def solution(mesh):
    in_specs = (
        P("dp", "tensor", None),
        P(("dp", "tensor")),
        P(("dp", "tensor")),
        P("dp", "tensor"),
        P("dp", "tensor"),
        P("dp", "tensor"),
        P("tensor", "dp"),
        P("dp", "tensor"),
        P("tensor", "dp", None),
        P("tensor", "dp", None),
        P("tensor", "dp", None),
        P("dp", "tensor", None),
        P("dp", None),
        P("dp", "tensor", None),
    )
    out_specs = (
        P("dp", "tensor", None),
        P("dp", "tensor", None),
        P(("dp", "tensor")),
        P(("dp", "tensor")),
        P("dp", "tensor"),
        P("dp", "tensor"),
        P("dp", "tensor"),
        P("tensor", "dp"),
        P("dp", "tensor"),
        P("tensor", "dp", None),
        P("tensor", "dp", None),
        P("tensor", "dp", None),
    )
    return jax.shard_map(
        on_device, mesh=mesh, in_specs=in_specs, out_specs=out_specs, check_vma=False
    )
```

```python
import functools
import math

import jax
import jax.numpy as jnp
from jax import lax
from jax.experimental import pallas as pl
from jax.experimental.pallas import tpu as pltpu
from jax.sharding import PartitionSpec as P


HD = 64
K = 8


epsilon = 1e-06
theta_base = 10000.0
masked_value = -1e30


def rotary_tables(length, head_width):
    half = head_width // 2
    frequency = theta_base ** (-(jnp.arange(half, dtype=jnp.float32) * 2.0 / head_width))
    angle = jnp.arange(length, dtype=jnp.float32)[:, None] * frequency[None, :]
    return (jnp.cos(angle)[:, None, :], jnp.sin(angle)[:, None, :])


def rotate(values, cosines, sines):
    half = values.shape[-1] // 2
    first = values[..., :half]
    second = values[..., half:]
    return jnp.concatenate(
        [first * cosines - second * sines, second * cosines + first * sines], axis=-1
    )


def rotate_back(grads, cosines, sines):
    half = grads.shape[-1] // 2
    first = grads[..., :half]
    second = grads[..., half:]
    return jnp.concatenate(
        [first * cosines + second * sines, second * cosines - first * sines], axis=-1
    )


f32 = jnp.float32
bf16 = jnp.bfloat16
vmem_bytes = 56 * 1024 * 1024
DEPTH = 4
CHUNKS = 4
small_cost = pl.CostEstimate(flops=1, bytes_accessed=1, transcendentals=0)


def dot(a, b, left=1, right=0):
    return lax.dot_general(a, b, (((left,), (right,)), ((), ())), preferred_element_type=f32)


def expert_kernel(
    ties, own_ref, rank_ref, gate_ref, x_ref, c_ref, wg_ref, wu_ref, wd_ref, *refs
):
    mix_ref, back_ref, gg_ref, *grads_ref = refs[ties:]
    blocks, cap = mix_ref.shape[1], mix_ref.shape[2]
    length = rank_ref.shape[-1]
    width = x_ref.shape[1]
    hidden_width = wg_ref.shape[-1]
    groups, _, rows_each, _ = wg_ref.shape
    planes = groups // 2 // DEPTH
    wg = wg_ref[...].reshape(width, hidden_width)
    wu = wu_ref[...].reshape(width, hidden_width)
    wd = wd_ref[...].reshape(width, hidden_width)
    slots = lax.broadcasted_iota(jnp.int32, (cap, length), 0)
    picks, rows, grads, gate_rows = [], [], [], []
    for b in range(blocks):
        pick = slots == rank_ref[0, b]
        one_hot = pick.astype(f32).astype(bf16)
        picks.append(pick)
        rows.append(dot(one_hot, x_ref[b * length : (b + 1) * length, :]).astype(bf16))
        grads.append(dot(one_hot, c_ref[b * length : (b + 1) * length, :]))
        gate_rows.append(jnp.sum(jnp.where(pick, gate_ref[0, b], 0.0), axis=1, keepdims=True))
    buffer = jnp.concatenate(rows, axis=0)
    cotangent = jnp.concatenate(grads, axis=0)
    gate_row = jnp.concatenate(gate_rows, axis=0)
    gate_pre = dot(buffer, wg)
    up_pre = dot(buffer, wu)
    sigmoid = 1.0 / (1.0 + jnp.exp(-gate_pre))
    silu = gate_pre * sigmoid
    hidden = (silu * up_pre).astype(bf16)
    produced = dot(hidden, wd, 1, 1)
    gates_grad = jnp.sum(cotangent * produced, axis=1, keepdims=True)
    mix = (gate_row * produced).astype(bf16)
    picked_grad = (gate_row * cotangent).astype(bf16)
    hidden_grad = dot(picked_grad, wd)
    gate_grad = (hidden_grad * up_pre * (sigmoid * (1.0 + gate_pre * (1.0 - sigmoid)))).astype(bf16)
    up_grad = (hidden_grad * silu).astype(bf16)
    back = (dot(gate_grad, wg, 1, 1) + dot(up_grad, wu, 1, 1)).astype(bf16)
    for b in range(blocks):
        mix_ref[0, b] = mix[b * cap : (b + 1) * cap]
        back_ref[0, b] = back[b * cap : (b + 1) * cap]
        gg_ref[0, b] = jnp.sum(
            jnp.where(picks[b], gates_grad[b * cap : (b + 1) * cap], 0.0), axis=0, keepdims=True
        )
    own_place = own_ref[0]
    for kind, (a, g) in enumerate(((buffer, gate_grad), (buffer, up_grad), (picked_grad, hidden))):
        total = dot(a, g, 0, 0).astype(bf16).reshape(groups, rows_each, hidden_width)
        for plane in range(2 * planes):
            for relative in range(2 * planes):

                @pl.when(own_place ^ plane == relative)
                def store():
                    for z in range(DEPTH):
                        grads_ref[relative][z, 0, kind] = total[z * 2 * planes + plane]


def experts(own, rank, gates, tokens, cotangent, weights, base, capacity, after):
    count, blocks, _, length = rank.shape
    width = tokens.shape[1]
    groups, _, rows_each, hidden_width = weights.shape
    places = groups // DEPTH
    whole = lambda e, own: (0, 0)
    each = lambda e, own: (e, 0, 0, 0)
    weight = lambda kind: pl.BlockSpec(
        (groups, 1, rows_each, hidden_width), lambda e, own: (0, base + 3 * e + kind, 0, 0)
    )
    grad = pl.BlockSpec((DEPTH, 1, 3, rows_each, hidden_width), lambda e, own: (0, e, 0, 0, 0))
    row = pl.BlockSpec((1, blocks, 1, length), each)
    moved = pl.BlockSpec((1, blocks, capacity, width), each)
    slots = jax.ShapeDtypeStruct((count, blocks, capacity, width), bf16)
    grads = jax.ShapeDtypeStruct((DEPTH, count, 3, rows_each, hidden_width), bf16)
    mix, back, gate_sum, *sums = pl.pallas_call(
        functools.partial(expert_kernel, len(after)),
        grid_spec=pltpu.PrefetchScalarGridSpec(
            num_scalar_prefetch=1,
            grid=(count,),
            in_specs=[
                row,
                row,
                pl.BlockSpec(tokens.shape, whole),
                pl.BlockSpec(tokens.shape, whole),
                weight(0),
                weight(1),
                weight(2),
            ]
            + [pl.BlockSpec(memory_space=pl.ANY)] * len(after),
            out_specs=[moved, moved, row] + [grad] * places,
        ),
        out_shape=[slots, slots, jax.ShapeDtypeStruct(rank.shape, f32)] + [grads] * places,
        compiler_params=pltpu.CompilerParams(vmem_limit_bytes=vmem_bytes),
        cost_estimate=small_cost,
    )(own, rank, gates, tokens, cotangent, weights, weights, weights, *after)
    return mix, back, gate_sum, sums


def combine_kernel(chunks, rank_ref, *refs):
    parts, mix_out, back_out = refs[: 2 * chunks], refs[-2], refs[-1]
    half = len(parts) // 2
    count, _, cap, tile = parts[0].shape
    length = rank_ref.shape[-1]
    slots = lax.broadcasted_iota(jnp.int32, (cap, length), 0)
    for sources, target in ((parts[:half], mix_out), (parts[half:], back_out)):
        total = jnp.zeros((length, tile), f32)
        for i, source in enumerate(sources):
            pick = jnp.concatenate(
                [
                    (slots == rank_ref[i * count + e, 0]).astype(f32).astype(bf16)
                    for e in range(count)
                ],
                axis=0,
            )
            total = total + dot(pick, source[...].reshape(count * cap, tile), 0, 0)
        target[...] = total.astype(bf16)


def combine(rank, mixes, backs, *after):
    experts_here, blocks, _, length = rank.shape
    count, _, cap, width = mixes[0].shape
    tile = min(512, width)
    source = pl.BlockSpec((count, 1, cap, tile), lambda b, n: (0, b, 0, n))
    target = pl.BlockSpec((length, tile), lambda b, n: (b, n))
    shape = jax.ShapeDtypeStruct((blocks * length, width), bf16)
    return pl.pallas_call(
        functools.partial(combine_kernel, len(mixes)),
        grid=(blocks, width // tile),
        in_specs=[pl.BlockSpec((experts_here, 1, 1, length), lambda b, n: (0, b, 0, 0))]
        + [source] * (2 * len(mixes))
        + [pl.BlockSpec(memory_space=pl.ANY)] * len(after),
        out_specs=[target, target],
        out_shape=[shape, shape],
        compiler_params=pltpu.CompilerParams(vmem_limit_bytes=vmem_bytes),
        cost_estimate=small_cost,
    )(rank, *mixes, *backs, *after)


def gather_tensor(piece):
    if lax.axis_size("tensor") != 2:
        return lax.all_gather(piece, "tensor", axis=0, tiled=True)
    other = lax.ppermute(piece, "tensor", [(0, 1), (1, 0)])
    first = lax.axis_index("tensor") == 0
    return jnp.concatenate([jnp.where(first, piece, other), jnp.where(first, other, piece)], axis=0)


def scatter_tensor(whole):
    if lax.axis_size("tensor") != 2:
        return lax.psum_scatter(
            whole.astype(bf16), "tensor", scatter_dimension=0, tiled=True
        ).astype(f32)
    length = whole.shape[0] // 2
    here = lax.axis_index("tensor")
    other = lax.dynamic_slice_in_dim(whole, (1 - here) * length, length, 0).astype(bf16)
    own = lax.dynamic_slice_in_dim(whole, here * length, length, 0)
    return own.astype(f32) + lax.ppermute(other, "tensor", [(0, 1), (1, 0)]).astype(f32)


def sum_tensor(array):
    if lax.axis_size("tensor") != 2:
        return lax.psum(array, "tensor")
    return array + lax.ppermute(array, "tensor", [(0, 1), (1, 0)])


def gather_experts(piece):
    parts, count, length = piece.shape
    if parts != 2:
        moved = lax.all_to_all(piece, "tensor", split_axis=0, concat_axis=0, tiled=True)
        return moved.reshape(parts * count, length)
    here = lax.axis_index("tensor")
    own = lax.dynamic_index_in_dim(piece, here, 0, keepdims=False)
    other = lax.dynamic_index_in_dim(piece, 1 - here, 0, keepdims=False)
    other = lax.ppermute(other, "tensor", [(0, 1), (1, 0)])
    first = here == 0
    return jnp.concatenate([jnp.where(first, own, other), jnp.where(first, other, own)], axis=0)


def swap(array, distance):
    return lax.ppermute(
        array, "dp", [(i, i ^ distance) for i in range(lax.axis_size("dp"))]
    ).astype(f32)


def sum_cores(sums):
    return [
        (sums[i].astype(f32) + swap(sums[i + 1], 1)).astype(bf16) for i in range(0, len(sums), 2)
    ]


def sum_rows(sums, *after):
    if after:
        sums = [tied(sums[0], *after)] + sums[1:]
    while len(sums) > 1:
        half = len(sums) // 2
        sums = [(sums[i].astype(f32) + swap(sums[half + i], 2 * half)).astype(bf16) for i in range(half)]
    return sums[0]


def sum_lines(array):
    plane = lax.axis_size("dp") // DEPTH
    lines = [[z * plane + i for z in range(DEPTH)] for i in range(plane)]
    return lax.psum_scatter(
        array, "dp", scatter_dimension=0, axis_index_groups=lines, tiled=False
    )


def tied(array, *after):
    def kernel(*refs):
        del refs

    anywhere = pl.BlockSpec(memory_space=pl.ANY)
    return pl.pallas_call(
        kernel,
        in_specs=[anywhere] * (1 + len(after)),
        out_specs=anywhere,
        out_shape=jax.ShapeDtypeStruct(array.shape, array.dtype),
        input_output_aliases={0: 0},
        cost_estimate=small_cost,
    )(array, *after)


def on_device(
    tokens,
    gain_attn,
    gain_ffn,
    w_query,
    w_key,
    w_value,
    w_out,
    router,
    w_gate,
    w_up,
    w_down,
    cotangent,
    segments,
    routing,
):
    _, local_len, width = tokens.shape
    parts = lax.axis_size("tensor")
    groups = lax.axis_size("dp")
    here = lax.axis_index("tensor")
    full_len = local_len * parts
    heads_here = w_query.shape[1] // HD
    kv_here = w_key.shape[1] // HD
    group_size = heads_here // kv_here
    experts_here = w_gate.shape[0]
    all_experts = experts_here * parts
    capacity = 17 * local_len * K // (16 * all_experts) + 1
    capacity = -(-capacity // 16) * 16
    gain_len = gain_attn.shape[0]
    rows_each = width // groups
    query_cols = heads_here * HD
    kv_cols = kv_here * HD
    scale = 1.0 / math.sqrt(HD)
    block = min(512, full_len)
    tokens = tokens[0]
    cotangent = cotangent[0]
    segments = segments[0]

    columns = jnp.zeros((rows_each, 2), bf16)
    columns = lax.dynamic_update_slice(
        columns, jnp.stack([gain_attn, gain_ffn], axis=1), (here * gain_len, 0)
    )
    small = gather_tensor(jnp.concatenate([router, columns], axis=1)[None])
    router_rows = jnp.transpose(small[:, :, :experts_here], (1, 0, 2)).reshape(rows_each, all_experts)
    gains_rows = jnp.sum(small[:, :, experts_here:].astype(f32), axis=0).astype(bf16)
    attention_piece = jnp.concatenate(
        [w_query, w_key, w_value, jnp.transpose(w_out), router_rows, gains_rows], axis=1
    )
    piece_cols = attention_piece.shape[1]
    hidden_width = w_gate.shape[2]
    attention_piece = jnp.pad(attention_piece, ((0, 0), (0, -piece_cols % hidden_width)))
    attention_blocks = attention_piece.shape[1] // hidden_width
    attention_piece = jnp.transpose(
        attention_piece.reshape(rows_each, attention_blocks, hidden_width), (1, 0, 2)
    )
    chunk = max(1, experts_here // CHUNKS)
    stacked = jnp.stack([w_gate, w_up, w_down], axis=1)
    stacked = stacked.reshape(3 * experts_here, rows_each, hidden_width)
    early = experts_here // 2
    first_weights = lax.all_gather(
        jnp.concatenate([attention_piece, stacked[: 3 * early]], axis=0), "dp", axis=0
    )
    second_weights = lax.all_gather(stacked[3 * early :], "dp", axis=0)
    attention_weights = jnp.concatenate(
        [first_weights[:, i].reshape(width, hidden_width) for i in range(attention_blocks)], axis=1
    )
    qkv_cols = query_cols + 2 * kv_cols
    qkv_weights = attention_weights[:, :qkv_cols]
    out_turned = attention_weights[:, qkv_cols : qkv_cols + query_cols]
    rest = attention_weights[:, qkv_cols + query_cols :]
    router_complete = rest[:, :all_experts]
    gain_one = rest[:, all_experts].astype(f32)
    gain_two = rest[:, all_experts + 1].astype(f32)

    cotangent_all = gather_tensor(cotangent.astype(bf16))
    routing_all = gather_tensor(routing[0])
    named = jnp.any(
        routing_all[:, :, None] == jnp.arange(all_experts, dtype=jnp.int32), axis=1
    )
    earlier = jnp.arange(local_len)[:, None] < jnp.arange(local_len)[None, :]
    named_here = lax.dynamic_slice_in_dim(named, here * experts_here, experts_here, 1)
    named_here = named_here.reshape(parts, local_len, experts_here)
    slots = jnp.einsum(
        "bte,ts->ebs", named_here.astype(bf16), earlier.astype(bf16), preferred_element_type=f32
    ).astype(jnp.int32)
    rank = jnp.where(jnp.transpose(named_here, (2, 0, 1)), slots, -1)[:, :, None, :]
    tokens_all = tied(gather_tensor(tokens), cotangent_all, rank)
    tokens_wide = tokens_all.astype(f32)
    inverse_one = lax.rsqrt(jnp.mean(tokens_wide * tokens_wide, axis=-1, keepdims=True) + epsilon)
    normalized_input = (tokens_wide * inverse_one * gain_one).astype(bf16)
    cosines, sines = rotary_tables(full_len, HD)
    qkv = dot(normalized_input, qkv_weights)
    queries = rotate(
        qkv[:, :query_cols].reshape(full_len, heads_here, HD), cosines, sines
    ).astype(bf16)
    keys = rotate(
        qkv[:, query_cols : query_cols + kv_cols].reshape(full_len, kv_here, HD), cosines, sines
    ).astype(bf16)
    values = qkv[:, query_cols + kv_cols :].reshape(full_len, kv_here, HD).astype(bf16)
    positions = jnp.arange(full_len, dtype=jnp.int32)

    def allowed_block(first, last):
        rows = positions[first : first + block]
        causal = rows[:, None] >= positions[None, :last]
        same = segments[first : first + block, None] == segments[None, :last]
        return causal & same

    head_outputs = []
    log_totals = []
    for head in range(heads_here):
        keys_head = keys[:, head // group_size]
        values_head = values[:, head // group_size]
        out_blocks = []
        total_blocks = []
        for first in range(0, full_len, block):
            last = min(first + block, full_len)
            score = dot(queries[first:last, head], keys_head[:last], 1, 1) * scale
            score = jnp.where(allowed_block(first, last), score, masked_value)
            top = jnp.max(score, axis=-1, keepdims=True)
            raised = jnp.exp(score - top)
            total = jnp.sum(raised, axis=-1, keepdims=True)
            probs = (raised / total).astype(bf16)
            out_blocks.append(dot(probs, values_head[:last]).astype(bf16))
            total_blocks.append(top + jnp.log(total))
        head_outputs.append(jnp.concatenate(out_blocks, axis=0))
        log_totals.append(jnp.concatenate(total_blocks, axis=0))
    mixed = jnp.concatenate(head_outputs, axis=-1)
    attended = scatter_tensor(dot(mixed, out_turned, 1, 1))
    tokens_local = tokens.astype(f32)
    residual = tokens_local + attended
    inverse_two = lax.rsqrt(jnp.mean(residual * residual, axis=-1, keepdims=True) + epsilon)
    normalized = (residual * inverse_two * gain_two).astype(bf16)
    normalized_all = gather_tensor(normalized)

    logits = dot(normalized_all, router_complete)
    chosen = jnp.where(named, logits, masked_value)
    raised = jnp.where(named, jnp.exp(chosen - jnp.max(chosen, axis=-1, keepdims=True)), 0.0)
    gates = raised / jnp.sum(raised, axis=-1, keepdims=True)
    gates_here = lax.dynamic_slice_in_dim(gates, here * experts_here, experts_here, 1)
    gates_here = jnp.transpose(gates_here).reshape(experts_here, parts, 1, local_len)

    own = (lax.axis_index("dp") % (groups // DEPTH)).astype(jnp.int32)[None]
    spans = [slice(first, first + chunk) for first in range(0, experts_here, chunk)]
    done = []

    def run(i, *after):
        first = spans[i].start
        weights, base = first_weights, attention_blocks + 3 * first
        if first >= early:
            weights, base = second_weights, 3 * (first - early)
        result = experts(
            own,
            rank[spans[i]],
            gates_here[spans[i]],
            normalized_all,
            cotangent_all,
            weights,
            base,
            capacity,
            after,
        )
        done.append(result[:3])
        return result[3]

    grads_0 = run(0, own)
    planes_0 = jnp.stack(sum_cores(grads_0), axis=1)
    lines_0 = sum_lines(planes_0)
    grads_1 = run(1, planes_0)
    cores_1 = sum_cores(grads_1)
    grads_2 = run(2, *cores_1)
    grads_3 = run(3, done[2][2])
    planes_2 = jnp.stack(sum_cores(grads_2), axis=1)
    gate_sums = [d[2] for d in done]
    rows_1 = sum_rows(cores_1, gate_sums[3])
    lines_1 = sum_lines(rows_1)
    mix_part, back_part = combine(
        rank, [d[0] for d in done], [d[1] for d in done], rows_1, planes_2
    )
    lines_2 = sum_lines(planes_2)
    cores_3 = sum_cores(grads_3)
    gate_sums = jnp.concatenate(gate_sums, axis=0).reshape(experts_here, parts, local_len)
    gates_grad = jnp.transpose(
        gather_experts(jnp.transpose(gate_sums, (1, 0, 2))), (1, 0)
    )
    ffn_grad = scatter_tensor(back_part)
    gates_local = lax.dynamic_slice_in_dim(gates, here * local_len, local_len, 0)
    selected_grad = gates_local * (
        gates_grad - jnp.sum(gates_local * gates_grad, axis=-1, keepdims=True)
    )
    logits_grad = selected_grad.astype(bf16)
    ffn_grad = ffn_grad + dot(logits_grad, router_complete, 1, 1)
    router_part = dot(normalized, logits_grad, 0, 0)
    hat_two = residual * inverse_two
    scaled_two = ffn_grad * gain_two
    residual_grad = cotangent + inverse_two * (
        scaled_two - hat_two * jnp.mean(hat_two * scaled_two, axis=-1, keepdims=True)
    )
    gain_two_part = jnp.sum(ffn_grad * hat_two, axis=0)
    gradient = gather_tensor(tied(residual_grad.astype(bf16), *cores_3, lines_0))
    output = (residual + scatter_tensor(tied(mix_part, gradient))).astype(bf16)

    mixed_grad = dot(gradient, out_turned).astype(bf16)
    out_grad_turned = dot(gradient, mixed, 0, 0)
    rows_3 = sum_rows(cores_3, mixed_grad)
    lines_3 = sum_lines(rows_3)
    mixed_grads = [mixed_grad[:, : heads_here // 2 * HD]]
    query_grads = []
    key_grads = [jnp.zeros((full_len, HD), f32) for _ in range(kv_here)]
    value_grads = [jnp.zeros((full_len, HD), f32) for _ in range(kv_here)]
    for head in range(heads_here):
        group = head // group_size
        if head == heads_here // 2:
            mixed_grads.append(tied(mixed_grad[:, head * HD :], rows_3, lines_1))
        keys_head = keys[:, group]
        values_head = values[:, group]
        blocks_grad = []
        for first in range(0, full_len, block):
            last = min(first + block, full_len)
            query_block = queries[first:last, head]
            score = dot(query_block, keys_head[:last], 1, 1) * scale
            score = jnp.where(allowed_block(first, last), score, masked_value)
            probs = jnp.exp(score - log_totals[head][first:last])
            column = head % (heads_here // 2) * HD
            out_grad_block = mixed_grads[-1][first:last, column : column + HD]
            prob_grad = dot(out_grad_block, values_head[:last], 1, 1)
            delta = jnp.sum(probs * prob_grad, axis=-1, keepdims=True)
            score_grad = (probs * (prob_grad - delta)).astype(bf16)
            blocks_grad.append(dot(score_grad, keys_head[:last]) * scale)
            key_grads[group] = (
                key_grads[group].at[:last].add(dot(score_grad, query_block, 0, 0) * scale)
            )
            value_grads[group] = (
                value_grads[group].at[:last].add(dot(probs.astype(bf16), out_grad_block, 0, 0))
            )
        query_grads.append(jnp.concatenate(blocks_grad, axis=0))
    query_gradient = rotate_back(jnp.stack(query_grads, axis=1), cosines, sines)
    key_gradient = rotate_back(jnp.stack(key_grads, axis=1), cosines, sines)
    qkv_gradient = jnp.concatenate(
        [
            query_gradient.astype(bf16).reshape(full_len, query_cols),
            key_gradient.astype(bf16).reshape(full_len, kv_cols),
            jnp.stack(value_grads, axis=1).astype(bf16).reshape(full_len, kv_cols),
        ],
        axis=1,
    )
    normed_grad = dot(qkv_gradient, qkv_weights, 1, 1)
    gain_one_part = jnp.sum(normed_grad * tokens_wide * inverse_one, axis=0)
    qkv_weight_grad = dot(normalized_input, qkv_gradient, 0, 0)
    row_sum = scatter_tensor(tied(normed_grad, lines_2, output))
    inverse_local = lax.rsqrt(
        jnp.mean(tokens_local * tokens_local, axis=-1, keepdims=True) + epsilon
    )
    hat_one = tokens_local * inverse_local
    scaled_one = row_sum * gain_one
    tokens_grad = (
        residual_grad
        + inverse_local
        * (scaled_one - hat_one * jnp.mean(hat_one * scaled_one, axis=-1, keepdims=True))
    ).astype(bf16)
    rest_grads = jnp.concatenate(
        [router_part, jnp.stack([gain_one_part, gain_two_part], axis=1)], axis=1
    ).astype(bf16)
    rest_grads = jnp.pad(rest_grads, ((0, 0), (0, -rest_grads.shape[1] % 128)))
    attention_grads = jnp.concatenate(
        [qkv_weight_grad.astype(bf16), out_grad_turned.astype(bf16), rest_grads], axis=1
    )
    plane = groups // DEPTH
    attention_grads = attention_grads.reshape(DEPTH, plane, rows_each, -1)
    attention_rows = sum_rows(
        sum_cores(
            [
                lax.dynamic_index_in_dim(attention_grads, own[0] ^ i, 1, keepdims=False)
                for i in range(plane)
            ]
        )
    )
    summed = sum_lines(tied(attention_rows, lines_3)).astype(f32)
    small_sum = sum_tensor(summed[:, qkv_cols + query_cols :])
    router_shard = lax.dynamic_slice_in_dim(small_sum, here * experts_here, experts_here, 1)
    gain_shard = lax.dynamic_slice_in_dim(small_sum, here * gain_len, gain_len, 0)
    rows_0, rows_2 = [
        sum_rows([lines[i] for i in range(plane // 2)]) for lines in (lines_0, lines_2)
    ]
    weight_grads = jnp.concatenate([rows_0, lines_1, rows_2, lines_3], axis=0).astype(f32)
    weight_grads = jnp.transpose(weight_grads, (1, 0, 2, 3))
    return (
        output[None],
        tokens_grad[None],
        gain_shard[:, all_experts],
        gain_shard[:, all_experts + 1],
        summed[:, :query_cols],
        summed[:, query_cols : query_cols + kv_cols],
        summed[:, query_cols + kv_cols : qkv_cols],
        jnp.transpose(summed[:, qkv_cols : qkv_cols + query_cols]),
        router_shard,
        weight_grads[0],
        weight_grads[1],
        weight_grads[2],
    )


def solution(mesh):
    in_specs = (
        P("dp", "tensor", None),
        P(("dp", "tensor")),
        P(("dp", "tensor")),
        P("dp", "tensor"),
        P("dp", "tensor"),
        P("dp", "tensor"),
        P("tensor", "dp"),
        P("dp", "tensor"),
        P("tensor", "dp", None),
        P("tensor", "dp", None),
        P("tensor", "dp", None),
        P("dp", "tensor", None),
        P("dp", None),
        P("dp", "tensor", None),
    )
    out_specs = (
        P("dp", "tensor", None),
        P("dp", "tensor", None),
        P(("dp", "tensor")),
        P(("dp", "tensor")),
        P("dp", "tensor"),
        P("dp", "tensor"),
        P("dp", "tensor"),
        P("tensor", "dp"),
        P("dp", "tensor"),
        P("tensor", "dp", None),
        P("tensor", "dp", None),
        P("tensor", "dp", None),
    )
    return jax.shard_map(
        on_device, mesh=mesh, in_specs=in_specs, out_specs=out_specs, check_vma=False
    )
```

```python
import functools
import math

import jax
import jax.numpy as jnp
from jax import lax
from jax.experimental import pallas as pl
from jax.experimental.pallas import tpu as pltpu
from jax.sharding import PartitionSpec as P


HD = 64
K = 8


epsilon = 1e-06
theta_base = 10000.0
masked_value = -1e30


def rotary_tables(length, head_width):
    half = head_width // 2
    frequency = theta_base ** (-(jnp.arange(half, dtype=jnp.float32) * 2.0 / head_width))
    angle = jnp.arange(length, dtype=jnp.float32)[:, None] * frequency[None, :]
    return (jnp.cos(angle)[:, None, :], jnp.sin(angle)[:, None, :])


def rotate(values, cosines, sines):
    half = values.shape[-1] // 2
    first = values[..., :half]
    second = values[..., half:]
    return jnp.concatenate(
        [first * cosines - second * sines, second * cosines + first * sines], axis=-1
    )


def rotate_back(grads, cosines, sines):
    half = grads.shape[-1] // 2
    first = grads[..., :half]
    second = grads[..., half:]
    return jnp.concatenate(
        [first * cosines + second * sines, second * cosines - first * sines], axis=-1
    )


f32 = jnp.float32
bf16 = jnp.bfloat16
vmem_bytes = 56 * 1024 * 1024
DEPTH = 4
CHUNKS = 4
small_cost = pl.CostEstimate(flops=1, bytes_accessed=1, transcendentals=0)


def dot(a, b, left=1, right=0):
    return lax.dot_general(a, b, (((left,), (right,)), ((), ())), preferred_element_type=f32)


def expert_kernel(
    ties, own_ref, rank_ref, gate_ref, x_ref, c_ref, wg_ref, wu_ref, wd_ref, *refs
):
    mix_ref, back_ref, gg_ref, *grads_ref = refs[ties:]
    blocks, cap = mix_ref.shape[1], mix_ref.shape[2]
    length = rank_ref.shape[-1]
    width = x_ref.shape[1]
    hidden_width = wg_ref.shape[-1]
    groups, _, rows_each, _ = wg_ref.shape
    planes = groups // 2 // DEPTH
    wg = wg_ref[...].reshape(width, hidden_width)
    wu = wu_ref[...].reshape(width, hidden_width)
    wd = wd_ref[...].reshape(width, hidden_width)
    slots = lax.broadcasted_iota(jnp.int32, (cap, length), 0)
    picks, rows, grads, gate_rows = [], [], [], []
    for b in range(blocks):
        pick = slots == rank_ref[0, b]
        one_hot = pick.astype(f32).astype(bf16)
        picks.append(pick)
        rows.append(dot(one_hot, x_ref[b * length : (b + 1) * length, :]).astype(bf16))
        grads.append(dot(one_hot, c_ref[b * length : (b + 1) * length, :]))
        gate_rows.append(jnp.sum(jnp.where(pick, gate_ref[0, b], 0.0), axis=1, keepdims=True))
    buffer = jnp.concatenate(rows, axis=0)
    cotangent = jnp.concatenate(grads, axis=0)
    gate_row = jnp.concatenate(gate_rows, axis=0)
    gate_pre = dot(buffer, wg)
    up_pre = dot(buffer, wu)
    sigmoid = 1.0 / (1.0 + jnp.exp(-gate_pre))
    silu = gate_pre * sigmoid
    hidden = (silu * up_pre).astype(bf16)
    produced = dot(hidden, wd, 1, 1)
    gates_grad = jnp.sum(cotangent * produced, axis=1, keepdims=True)
    mix = (gate_row * produced).astype(bf16)
    picked_grad = (gate_row * cotangent).astype(bf16)
    hidden_grad = dot(picked_grad, wd)
    gate_grad = (hidden_grad * up_pre * (sigmoid * (1.0 + gate_pre * (1.0 - sigmoid)))).astype(bf16)
    up_grad = (hidden_grad * silu).astype(bf16)
    back = (dot(gate_grad, wg, 1, 1) + dot(up_grad, wu, 1, 1)).astype(bf16)
    for b in range(blocks):
        mix_ref[0, b] = mix[b * cap : (b + 1) * cap]
        back_ref[0, b] = back[b * cap : (b + 1) * cap]
        gg_ref[0, b] = jnp.sum(
            jnp.where(picks[b], gates_grad[b * cap : (b + 1) * cap], 0.0), axis=0, keepdims=True
        )
    own_place = own_ref[0]
    for kind, (a, g) in enumerate(((buffer, gate_grad), (buffer, up_grad), (picked_grad, hidden))):
        total = dot(a, g, 0, 0).astype(bf16).reshape(groups, rows_each, hidden_width)
        for plane in range(2 * planes):
            for relative in range(2 * planes):

                @pl.when(own_place ^ plane == relative)
                def store():
                    for z in range(DEPTH):
                        grads_ref[relative][z, 0, kind] = total[z * 2 * planes + plane]


def experts(own, rank, gates, tokens, cotangent, weights, base, capacity, after):
    count, blocks, _, length = rank.shape
    width = tokens.shape[1]
    groups, _, rows_each, hidden_width = weights.shape
    places = groups // DEPTH
    whole = lambda e, own: (0, 0)
    each = lambda e, own: (e, 0, 0, 0)
    weight = lambda kind: pl.BlockSpec(
        (groups, 1, rows_each, hidden_width), lambda e, own: (0, base + 3 * e + kind, 0, 0)
    )
    grad = pl.BlockSpec((DEPTH, 1, 3, rows_each, hidden_width), lambda e, own: (0, e, 0, 0, 0))
    row = pl.BlockSpec((1, blocks, 1, length), each)
    moved = pl.BlockSpec((1, blocks, capacity, width), each)
    slots = jax.ShapeDtypeStruct((count, blocks, capacity, width), bf16)
    grads = jax.ShapeDtypeStruct((DEPTH, count, 3, rows_each, hidden_width), bf16)
    mix, back, gate_sum, *sums = pl.pallas_call(
        functools.partial(expert_kernel, len(after)),
        grid_spec=pltpu.PrefetchScalarGridSpec(
            num_scalar_prefetch=1,
            grid=(count,),
            in_specs=[
                row,
                row,
                pl.BlockSpec(tokens.shape, whole),
                pl.BlockSpec(tokens.shape, whole),
                weight(0),
                weight(1),
                weight(2),
            ]
            + [pl.BlockSpec(memory_space=pl.ANY)] * len(after),
            out_specs=[moved, moved, row] + [grad] * places,
        ),
        out_shape=[slots, slots, jax.ShapeDtypeStruct(rank.shape, f32)] + [grads] * places,
        compiler_params=pltpu.CompilerParams(vmem_limit_bytes=vmem_bytes),
        cost_estimate=small_cost,
    )(own, rank, gates, tokens, cotangent, weights, weights, weights, *after)
    return mix, back, gate_sum, sums


def combine_kernel(chunks, rank_ref, *refs):
    parts, mix_out, back_out = refs[: 2 * chunks], refs[-2], refs[-1]
    half = len(parts) // 2
    count, _, cap, tile = parts[0].shape
    length = rank_ref.shape[-1]
    slots = lax.broadcasted_iota(jnp.int32, (cap, length), 0)
    for sources, target in ((parts[:half], mix_out), (parts[half:], back_out)):
        total = jnp.zeros((length, tile), f32)
        for i, source in enumerate(sources):
            pick = jnp.concatenate(
                [
                    (slots == rank_ref[i * count + e, 0]).astype(f32).astype(bf16)
                    for e in range(count)
                ],
                axis=0,
            )
            total = total + dot(pick, source[...].reshape(count * cap, tile), 0, 0)
        target[...] = total.astype(bf16)


def combine(rank, mixes, backs, *after):
    experts_here, blocks, _, length = rank.shape
    count, _, cap, width = mixes[0].shape
    tile = min(512, width)
    source = pl.BlockSpec((count, 1, cap, tile), lambda b, n: (0, b, 0, n))
    target = pl.BlockSpec((length, tile), lambda b, n: (b, n))
    shape = jax.ShapeDtypeStruct((blocks * length, width), bf16)
    return pl.pallas_call(
        functools.partial(combine_kernel, len(mixes)),
        grid=(blocks, width // tile),
        in_specs=[pl.BlockSpec((experts_here, 1, 1, length), lambda b, n: (0, b, 0, 0))]
        + [source] * (2 * len(mixes))
        + [pl.BlockSpec(memory_space=pl.ANY)] * len(after),
        out_specs=[target, target],
        out_shape=[shape, shape],
        compiler_params=pltpu.CompilerParams(vmem_limit_bytes=vmem_bytes),
        cost_estimate=small_cost,
    )(rank, *mixes, *backs, *after)


def gather_tensor(piece):
    if lax.axis_size("tensor") != 2:
        return lax.all_gather(piece, "tensor", axis=0, tiled=True)
    other = lax.ppermute(piece, "tensor", [(0, 1), (1, 0)])
    first = lax.axis_index("tensor") == 0
    return jnp.concatenate([jnp.where(first, piece, other), jnp.where(first, other, piece)], axis=0)


def scatter_tensor(whole):
    if lax.axis_size("tensor") != 2:
        return lax.psum_scatter(
            whole.astype(bf16), "tensor", scatter_dimension=0, tiled=True
        ).astype(f32)
    length = whole.shape[0] // 2
    here = lax.axis_index("tensor")
    other = lax.dynamic_slice_in_dim(whole, (1 - here) * length, length, 0).astype(bf16)
    own = lax.dynamic_slice_in_dim(whole, here * length, length, 0)
    return own.astype(f32) + lax.ppermute(other, "tensor", [(0, 1), (1, 0)]).astype(f32)


def sum_tensor(array):
    if lax.axis_size("tensor") != 2:
        return lax.psum(array, "tensor")
    return array + lax.ppermute(array, "tensor", [(0, 1), (1, 0)])


def gather_experts(piece):
    parts, count, length = piece.shape
    if parts != 2:
        moved = lax.all_to_all(piece, "tensor", split_axis=0, concat_axis=0, tiled=True)
        return moved.reshape(parts * count, length)
    here = lax.axis_index("tensor")
    own = lax.dynamic_index_in_dim(piece, here, 0, keepdims=False)
    other = lax.dynamic_index_in_dim(piece, 1 - here, 0, keepdims=False)
    other = lax.ppermute(other, "tensor", [(0, 1), (1, 0)])
    first = here == 0
    return jnp.concatenate([jnp.where(first, own, other), jnp.where(first, other, own)], axis=0)


def swap(array, distance):
    return lax.ppermute(
        array, "dp", [(i, i ^ distance) for i in range(lax.axis_size("dp"))]
    ).astype(f32)


def sum_cores(sums, *after):
    if after:
        sums = [tied(s, *after) if i % 2 == 0 else s for i, s in enumerate(sums)]
    return [
        (sums[i].astype(f32) + swap(sums[i + 1], 1)).astype(bf16) for i in range(0, len(sums), 2)
    ]


def sum_rows(sums, *after):
    if after:
        sums = [tied(sums[0], *after)] + sums[1:]
    while len(sums) > 1:
        half = len(sums) // 2
        sums = [(sums[i].astype(f32) + swap(sums[half + i], 2 * half)).astype(bf16) for i in range(half)]
    return sums[0]


def sum_lines(array):
    plane = lax.axis_size("dp") // DEPTH
    lines = [[z * plane + i for z in range(DEPTH)] for i in range(plane)]
    return lax.psum_scatter(
        array, "dp", scatter_dimension=0, axis_index_groups=lines, tiled=False
    )


def tied(array, *after):
    def kernel(*refs):
        del refs

    anywhere = pl.BlockSpec(memory_space=pl.ANY)
    return pl.pallas_call(
        kernel,
        in_specs=[anywhere] * (1 + len(after)),
        out_specs=anywhere,
        out_shape=jax.ShapeDtypeStruct(array.shape, array.dtype),
        input_output_aliases={0: 0},
        cost_estimate=small_cost,
    )(array, *after)


def on_device(
    tokens,
    gain_attn,
    gain_ffn,
    w_query,
    w_key,
    w_value,
    w_out,
    router,
    w_gate,
    w_up,
    w_down,
    cotangent,
    segments,
    routing,
):
    _, local_len, width = tokens.shape
    parts = lax.axis_size("tensor")
    groups = lax.axis_size("dp")
    here = lax.axis_index("tensor")
    full_len = local_len * parts
    heads_here = w_query.shape[1] // HD
    kv_here = w_key.shape[1] // HD
    group_size = heads_here // kv_here
    experts_here = w_gate.shape[0]
    all_experts = experts_here * parts
    capacity = 17 * local_len * K // (16 * all_experts) + 1
    capacity = -(-capacity // 16) * 16
    gain_len = gain_attn.shape[0]
    rows_each = width // groups
    query_cols = heads_here * HD
    kv_cols = kv_here * HD
    scale = 1.0 / math.sqrt(HD)
    block = min(512, full_len)
    tokens = tokens[0]
    cotangent = cotangent[0]
    segments = segments[0]

    columns = jnp.zeros((rows_each, 2), bf16)
    columns = lax.dynamic_update_slice(
        columns, jnp.stack([gain_attn, gain_ffn], axis=1), (here * gain_len, 0)
    )
    small = gather_tensor(jnp.concatenate([router, columns], axis=1)[None])
    router_rows = jnp.transpose(small[:, :, :experts_here], (1, 0, 2)).reshape(rows_each, all_experts)
    gains_rows = jnp.sum(small[:, :, experts_here:].astype(f32), axis=0).astype(bf16)
    attention_piece = jnp.concatenate(
        [w_query, w_key, w_value, jnp.transpose(w_out), router_rows, gains_rows], axis=1
    )
    piece_cols = attention_piece.shape[1]
    hidden_width = w_gate.shape[2]
    attention_piece = jnp.pad(attention_piece, ((0, 0), (0, -piece_cols % hidden_width)))
    attention_blocks = attention_piece.shape[1] // hidden_width
    attention_piece = jnp.transpose(
        attention_piece.reshape(rows_each, attention_blocks, hidden_width), (1, 0, 2)
    )
    chunk = max(1, experts_here // CHUNKS)
    stacked = jnp.stack([w_gate, w_up, w_down], axis=1)
    stacked = stacked.reshape(3 * experts_here, rows_each, hidden_width)
    early = experts_here // 2
    attention_gathered = lax.all_gather(attention_piece, "dp", axis=0)
    first_weights = lax.all_gather(
        tied(stacked[: 3 * early], attention_piece), "dp", axis=0
    )
    second_weights = lax.all_gather(stacked[3 * early :], "dp", axis=0)
    attention_weights = jnp.concatenate(
        [attention_gathered[:, i].reshape(width, hidden_width) for i in range(attention_blocks)], axis=1
    )
    qkv_cols = query_cols + 2 * kv_cols
    qkv_weights = attention_weights[:, :qkv_cols]
    out_turned = attention_weights[:, qkv_cols : qkv_cols + query_cols]
    rest = attention_weights[:, qkv_cols + query_cols :]
    router_complete = rest[:, :all_experts]
    gain_one = rest[:, all_experts].astype(f32)
    gain_two = rest[:, all_experts + 1].astype(f32)

    cotangent_all = gather_tensor(cotangent.astype(bf16))
    routing_all = gather_tensor(routing[0])
    named = jnp.any(
        routing_all[:, :, None] == jnp.arange(all_experts, dtype=jnp.int32), axis=1
    )
    earlier = jnp.arange(local_len)[:, None] < jnp.arange(local_len)[None, :]
    named_here = lax.dynamic_slice_in_dim(named, here * experts_here, experts_here, 1)
    named_here = named_here.reshape(parts, local_len, experts_here)
    slots = jnp.einsum(
        "bte,ts->ebs", named_here.astype(bf16), earlier.astype(bf16), preferred_element_type=f32
    ).astype(jnp.int32)
    rank = jnp.where(jnp.transpose(named_here, (2, 0, 1)), slots, -1)[:, :, None, :]
    tokens_all = tied(gather_tensor(tokens), cotangent_all, rank)
    tokens_wide = tokens_all.astype(f32)
    inverse_one = lax.rsqrt(jnp.mean(tokens_wide * tokens_wide, axis=-1, keepdims=True) + epsilon)
    normalized_input = (tokens_wide * inverse_one * gain_one).astype(bf16)
    cosines, sines = rotary_tables(full_len, HD)
    qkv = dot(normalized_input, qkv_weights)
    queries = rotate(
        qkv[:, :query_cols].reshape(full_len, heads_here, HD), cosines, sines
    ).astype(bf16)
    keys = rotate(
        qkv[:, query_cols : query_cols + kv_cols].reshape(full_len, kv_here, HD), cosines, sines
    ).astype(bf16)
    values = qkv[:, query_cols + kv_cols :].reshape(full_len, kv_here, HD).astype(bf16)
    positions = jnp.arange(full_len, dtype=jnp.int32)

    def allowed_block(first, last):
        rows = positions[first : first + block]
        causal = rows[:, None] >= positions[None, :last]
        same = segments[first : first + block, None] == segments[None, :last]
        return causal & same

    head_outputs = []
    log_totals = []
    for head in range(heads_here):
        keys_head = keys[:, head // group_size]
        values_head = values[:, head // group_size]
        out_blocks = []
        total_blocks = []
        for first in range(0, full_len, block):
            last = min(first + block, full_len)
            score = dot(queries[first:last, head], keys_head[:last], 1, 1) * scale
            score = jnp.where(allowed_block(first, last), score, masked_value)
            top = jnp.max(score, axis=-1, keepdims=True)
            raised = jnp.exp(score - top)
            total = jnp.sum(raised, axis=-1, keepdims=True)
            probs = (raised / total).astype(bf16)
            out_blocks.append(dot(probs, values_head[:last]).astype(bf16))
            total_blocks.append(top + jnp.log(total))
        head_outputs.append(jnp.concatenate(out_blocks, axis=0))
        log_totals.append(jnp.concatenate(total_blocks, axis=0))
    mixed = jnp.concatenate(head_outputs, axis=-1)
    attended = scatter_tensor(dot(mixed, out_turned, 1, 1))
    tokens_local = tokens.astype(f32)
    residual = tokens_local + attended
    inverse_two = lax.rsqrt(jnp.mean(residual * residual, axis=-1, keepdims=True) + epsilon)
    normalized = (residual * inverse_two * gain_two).astype(bf16)
    normalized_all = gather_tensor(normalized)

    logits = dot(normalized_all, router_complete)
    chosen = jnp.where(named, logits, masked_value)
    raised = jnp.where(named, jnp.exp(chosen - jnp.max(chosen, axis=-1, keepdims=True)), 0.0)
    gates = raised / jnp.sum(raised, axis=-1, keepdims=True)
    gates_here = lax.dynamic_slice_in_dim(gates, here * experts_here, experts_here, 1)
    gates_here = jnp.transpose(gates_here).reshape(experts_here, parts, 1, local_len)

    own = (lax.axis_index("dp") % (groups // DEPTH)).astype(jnp.int32)[None]
    spans = [slice(first, first + chunk) for first in range(0, experts_here, chunk)]
    done = []

    def run(i, *after):
        first = spans[i].start
        weights, base = first_weights, 3 * first
        if first >= early:
            weights, base = second_weights, 3 * (first - early)
        result = experts(
            own,
            rank[spans[i]],
            gates_here[spans[i]],
            normalized_all,
            cotangent_all,
            weights,
            base,
            capacity,
            after,
        )
        done.append(result[:3])
        return result[3]

    grads_0 = run(0, own)
    planes_0 = jnp.stack(sum_cores(grads_0), axis=1)
    lines_0 = sum_lines(planes_0)
    grads_1 = run(1, planes_0)
    cores_1 = sum_cores(grads_1, second_weights)
    grads_2 = run(2, *cores_1[len(cores_1) // 2 :])
    cores_2 = sum_cores(grads_2)
    grads_3 = run(3, *cores_2[len(cores_2) // 2 :])
    gate_sums = [d[2] for d in done]
    mix_part, back_part = combine(rank, [d[0] for d in done], [d[1] for d in done])
    rows_1 = sum_rows(cores_1, mix_part)
    lines_1 = sum_lines(rows_1)
    cores_3 = sum_cores(grads_3)
    gate_sums = jnp.concatenate(gate_sums, axis=0).reshape(experts_here, parts, local_len)
    gates_grad = jnp.transpose(
        gather_experts(jnp.transpose(gate_sums, (1, 0, 2))), (1, 0)
    )
    ffn_grad = scatter_tensor(back_part)
    gates_local = lax.dynamic_slice_in_dim(gates, here * local_len, local_len, 0)
    gates_local = tied(gates_local, rows_1, *cores_3)
    selected_grad = gates_local * (
        gates_grad - jnp.sum(gates_local * gates_grad, axis=-1, keepdims=True)
    )
    logits_grad = selected_grad.astype(bf16)
    ffn_grad = ffn_grad + dot(logits_grad, router_complete, 1, 1)
    router_part = dot(normalized, logits_grad, 0, 0)
    hat_two = residual * inverse_two
    scaled_two = ffn_grad * gain_two
    residual_grad = cotangent + inverse_two * (
        scaled_two - hat_two * jnp.mean(hat_two * scaled_two, axis=-1, keepdims=True)
    )
    gain_two_part = jnp.sum(ffn_grad * hat_two, axis=0)
    gradient = gather_tensor(tied(residual_grad.astype(bf16), *cores_3, lines_0))
    rows_2 = sum_rows(cores_2, gradient)
    lines_2 = sum_lines(rows_2)
    output = (residual + scatter_tensor(tied(mix_part, gradient))).astype(bf16)

    mixed_grad = tied(dot(gradient, out_turned).astype(bf16), rows_2, lines_1)
    out_grad_turned = dot(gradient, mixed, 0, 0)
    rows_3 = sum_rows(cores_3, mixed_grad)
    lines_3 = sum_lines(rows_3)
    query_grads = []
    key_grads = [jnp.zeros((full_len, HD), f32) for _ in range(kv_here)]
    value_grads = [jnp.zeros((full_len, HD), f32) for _ in range(kv_here)]
    for head in range(heads_here):
        group = head // group_size
        keys_head = keys[:, group]
        values_head = values[:, group]
        blocks_grad = []
        for first in range(0, full_len, block):
            last = min(first + block, full_len)
            query_block = queries[first:last, head]
            score = dot(query_block, keys_head[:last], 1, 1) * scale
            score = jnp.where(allowed_block(first, last), score, masked_value)
            probs = jnp.exp(score - log_totals[head][first:last])
            out_grad_block = mixed_grad[first:last, head * HD : (head + 1) * HD]
            prob_grad = dot(out_grad_block, values_head[:last], 1, 1)
            delta = jnp.sum(probs * prob_grad, axis=-1, keepdims=True)
            score_grad = (probs * (prob_grad - delta)).astype(bf16)
            blocks_grad.append(dot(score_grad, keys_head[:last]) * scale)
            key_grads[group] = (
                key_grads[group].at[:last].add(dot(score_grad, query_block, 0, 0) * scale)
            )
            value_grads[group] = (
                value_grads[group].at[:last].add(dot(probs.astype(bf16), out_grad_block, 0, 0))
            )
        query_grads.append(jnp.concatenate(blocks_grad, axis=0))
    query_gradient = rotate_back(jnp.stack(query_grads, axis=1), cosines, sines)
    key_gradient = rotate_back(jnp.stack(key_grads, axis=1), cosines, sines)
    qkv_gradient = jnp.concatenate(
        [
            query_gradient.astype(bf16).reshape(full_len, query_cols),
            key_gradient.astype(bf16).reshape(full_len, kv_cols),
            jnp.stack(value_grads, axis=1).astype(bf16).reshape(full_len, kv_cols),
        ],
        axis=1,
    )
    qkv_gradient = tied(qkv_gradient, rows_3)
    normed_grad = dot(qkv_gradient, qkv_weights, 1, 1)
    gain_one_part = jnp.sum(normed_grad * tokens_wide * inverse_one, axis=0)
    qkv_weight_grad = dot(normalized_input, qkv_gradient, 0, 0)
    row_sum = scatter_tensor(tied(normed_grad, lines_2, output))
    inverse_local = lax.rsqrt(
        jnp.mean(tokens_local * tokens_local, axis=-1, keepdims=True) + epsilon
    )
    hat_one = tokens_local * inverse_local
    scaled_one = row_sum * gain_one
    tokens_grad = (
        residual_grad
        + inverse_local
        * (scaled_one - hat_one * jnp.mean(hat_one * scaled_one, axis=-1, keepdims=True))
    ).astype(bf16)
    rest_grads = jnp.concatenate(
        [router_part, jnp.stack([gain_one_part, gain_two_part], axis=1)], axis=1
    ).astype(bf16)
    rest_grads = jnp.pad(rest_grads, ((0, 0), (0, -rest_grads.shape[1] % 128)))
    attention_grads = jnp.concatenate(
        [qkv_weight_grad.astype(bf16), out_grad_turned.astype(bf16), rest_grads], axis=1
    )
    plane = groups // DEPTH
    attention_grads = attention_grads.reshape(DEPTH, plane, rows_each, -1)
    attention_rows = sum_rows(
        sum_cores(
            [
                lax.dynamic_index_in_dim(attention_grads, own[0] ^ i, 1, keepdims=False)
                for i in range(plane)
            ]
        )
    )
    summed = sum_lines(tied(attention_rows, lines_3)).astype(f32)
    small_sum = sum_tensor(summed[:, qkv_cols + query_cols :])
    router_shard = lax.dynamic_slice_in_dim(small_sum, here * experts_here, experts_here, 1)
    gain_shard = lax.dynamic_slice_in_dim(small_sum, here * gain_len, gain_len, 0)
    lines_0 = tied(lines_0, attention_rows)
    rows_0 = sum_rows([lines_0[i] for i in range(plane // 2)])
    weight_grads = jnp.concatenate([rows_0, lines_1, lines_2, lines_3], axis=0).astype(f32)
    weight_grads = jnp.transpose(weight_grads, (1, 0, 2, 3))
    return (
        output[None],
        tokens_grad[None],
        gain_shard[:, all_experts],
        gain_shard[:, all_experts + 1],
        summed[:, :query_cols],
        summed[:, query_cols : query_cols + kv_cols],
        summed[:, query_cols + kv_cols : qkv_cols],
        jnp.transpose(summed[:, qkv_cols : qkv_cols + query_cols]),
        router_shard,
        weight_grads[0],
        weight_grads[1],
        weight_grads[2],
    )


def solution(mesh):
    in_specs = (
        P("dp", "tensor", None),
        P(("dp", "tensor")),
        P(("dp", "tensor")),
        P("dp", "tensor"),
        P("dp", "tensor"),
        P("dp", "tensor"),
        P("tensor", "dp"),
        P("dp", "tensor"),
        P("tensor", "dp", None),
        P("tensor", "dp", None),
        P("tensor", "dp", None),
        P("dp", "tensor", None),
        P("dp", None),
        P("dp", "tensor", None),
    )
    out_specs = (
        P("dp", "tensor", None),
        P("dp", "tensor", None),
        P(("dp", "tensor")),
        P(("dp", "tensor")),
        P("dp", "tensor"),
        P("dp", "tensor"),
        P("dp", "tensor"),
        P("tensor", "dp"),
        P("dp", "tensor"),
        P("tensor", "dp", None),
        P("tensor", "dp", None),
        P("tensor", "dp", None),
    )
    return jax.shard_map(
        on_device, mesh=mesh, in_specs=in_specs, out_specs=out_specs, check_vma=False
    )
```
